256 devices in a mesh: seq: 4 (over y), vocab: 64 (over z, x, core).
Axes of the slice: x: 4, y: 4, z: 8, core: 2. Of those that a mesh axis runs over, the one named last changes fastest.
Arguments:
- hidden: bfloat16 [2048, 2048], P('seq', 'vocab')
- tangent: bfloat16 [2048, 2048], P('seq', 'vocab'), may hold values from -6 to 6
- head_weight: bfloat16 [2048, 76032], P(None, 'vocab'), as said below
- weight_dir: bfloat16 [2048, 76032], P(None, 'vocab'), may hold values from -0.125 to 0.125
Outputs:
- grad_hidden: float32 [2048, 2048], P('seq', 'vocab')
- grad_weight: float32 [2048, 76032], P('seq', 'vocab')
The draws below stay inside these ranges and needn't reach their ends.
Inputs may be any that keep to these rules, and one draw needn't show every extreme that they name: `head_weight`: columns of the head have scales of order one that differ between entries.
All inputs are finite; a program needn't handle non-finite values.
Results may differ from the reference program's by a relative error of at most 0.0029.
Values may be sent and summed in bfloat16 or wider, within the bound.
No kernel may reach another device: no remote copies, remote signals or barrier semaphores. Data moves between devices by JAX's collectives and lax.ppermute only.
A program may use at most 128 MiB of HBM per device.

```python
import jax
import jax.numpy as jnp
from jax import lax

D = 2048
VOCAB = 76032
TOKENS = 2048


def weight_base(key):
    normal_key, scale_key = jax.random.split(jax.random.fold_in(key, 11))
    values = jax.random.normal(normal_key, (D, VOCAB), jnp.float32)
    place = jnp.arange(VOCAB, dtype=jnp.float32) / VOCAB
    spread = jnp.exp(jax.random.uniform(scale_key, (VOCAB,), jnp.float32, -1.4, 0.9))
    column_scale = jnp.exp(0.2 * (place - 0.5)) * spread
    return values * (1.0 / jnp.sqrt(float(D))) * column_scale[None, :]


def draw_head_weight(key, part):
    return weight_base(key).astype(jnp.bfloat16)


def draw_hidden(key, part):
    own = jax.random.fold_in(key, 5)
    rows = jax.random.normal(own, (TOKENS, D), jnp.float32)
    rows = jnp.clip(rows, -6.0, 6.0)
    return rows.astype(jnp.bfloat16)


def block_scale(rng, dims, cuts, low, largest):
    factor_of, own = 1.0, jax.random.fold_in(rng, 6)
    for axis_at, parts in cuts:
        steps = jnp.exp(jax.random.uniform(jax.random.fold_in(own, axis_at), (parts,), jnp.float32, low / len(cuts), largest / len(cuts)))
        factor_of = factor_of * jnp.repeat(steps, dims[axis_at] // parts).reshape([-1 if axis == axis_at else 1 for axis in range(len(dims))])
    return factor_of


def scatter_about(stream_key, shape, width, reach, shards=(), kind=jnp.bfloat16):
    result = width * jax.random.normal(stream_key, shape, jnp.float32)
    if shards:
        result = result * block_scale(stream_key, shape, shards, -0.22, 0.18)
    return jnp.clip(result, -reach, reach).astype(kind)


def setup_inputs(seed: int = 0) -> dict:
    key_list = jax.random.split(jax.random.key(seed), 5)
    return {
        "hidden": draw_hidden(jax.random.fold_in(key_list[4], 71), 0),
        "tangent": scatter_about(key_list[1], (TOKENS, D), 1.0, 6.0, ((0, 4), (1, 64))),
        "head_weight": draw_head_weight(jax.random.fold_in(key_list[4], 71), 0),
        "weight_dir": scatter_about(key_list[3], (D, VOCAB), D ** -0.5, 0.125, ((1, 64),)),
    }


def reference(hidden, tangent, head_weight, weight_dir):
    block = min(256, TOKENS)
    count = TOKENS // block
    hidden_blocks = hidden.reshape(count, block, D)
    tangent_blocks = tangent.reshape(count, block, D)

    def step(carry, pair):
        rows, tangents = pair
        logits = jnp.dot(rows, head_weight, preferred_element_type=jnp.float32)
        moved = jnp.dot(tangents, head_weight, preferred_element_type=jnp.float32) + jnp.dot(rows, weight_dir, preferred_element_type=jnp.float32)
        top = jnp.max(logits, axis=1, keepdims=True)
        scaled = jnp.exp(logits - top)
        total = jnp.sum(scaled, axis=1, keepdims=True)
        weighted = jnp.sum(scaled * moved, axis=1, keepdims=True)
        probe = (scaled / total * (moved - weighted / total)).astype(jnp.bfloat16)
        grad_rows = lax.dot_general(probe, head_weight, (((1,), (1,)), ((), ())), preferred_element_type=jnp.float32)
        carry = carry + lax.dot_general(rows, probe, (((0,), (0,)), ((), ())), preferred_element_type=jnp.float32)
        return carry, grad_rows

    start = jnp.zeros((D, VOCAB), jnp.float32)
    grad_weight, grad_rows = lax.scan(step, start, (hidden_blocks, tangent_blocks))
    return grad_rows.reshape(TOKENS, D), grad_weight
```

```python
import jax
import jax.numpy as jnp
from jax import lax
from jax.experimental import pallas as pl
from jax.experimental.pallas import tpu as pltpu
from jax.sharding import PartitionSpec as P

NZ, NX, NC, NY = 8, 4, 2, 4
F32, BF16 = jnp.float32, jnp.bfloat16
BLOCK = 304


def vocab_shift(a, dim, k):
    perm = []
    for z in range(NZ):
        for x in range(NX):
            for c in range(NC):
                at = [z, x, c]
                at[dim] = (at[dim] + k) % (NZ, NX, NC)[dim]
                perm.append(((at[0] * NX + at[1]) * NC + at[2], (z * NX + x) * NC + c))
    return lax.ppermute(a, "vocab", perm)


def seq_shift(a, k):
    return lax.ppermute(a, "seq", [((y + k) % NY, y) for y in range(NY)])


def order_kernel(pos_ref, own_ref, other_ref, h_ref, t_ref):
    z, x, c = pos_ref[0], pos_ref[1], pos_ref[2]
    for kc, src in enumerate((own_ref, other_ref)):
        for kx in range(NX):
            for kz in range(NZ):
                zz = lax.rem(z + kz, NZ)
                xx = lax.rem(x + kx, NX)
                cc = lax.rem(c + kc, NC)
                row = pl.multiple_of(zz * 256 + xx * 64 + cc * 32, 32)
                h_ref[pl.ds(row, 32), :] = src[kx, kz, 0:32, :]
                t_ref[pl.ds(row, 32), :] = src[kx, kz, 32:64, :]


def order(pos, own, other, d, t):
    return pl.pallas_call(
        order_kernel,
        out_shape=(jax.ShapeDtypeStruct((d, t), BF16),) * 2,
        in_specs=[pl.BlockSpec(memory_space=pltpu.SMEM)] + [pl.BlockSpec(memory_space=pltpu.VMEM)] * 2,
        out_specs=(pl.BlockSpec(memory_space=pltpu.VMEM),) * 2,
        compiler_params=pltpu.CompilerParams(vmem_limit_bytes=40 * 2**20),
    )(pos, own, other)


def fwd_kernel(n, h_ref, t_ref, w_ref, d_ref, l_ref, m_ref, s_ref):
    i = pl.program_id(0)
    w = w_ref[...]
    h = h_ref[...]
    logits = jnp.dot(w, h, preferred_element_type=F32)
    moved = jnp.dot(w, t_ref[...], preferred_element_type=F32) + jnp.dot(
        d_ref[...], h, preferred_element_type=F32
    )
    row = lax.broadcasted_iota(jnp.int32, logits.shape, 0) + i * BLOCK
    logits = jnp.where(row < n, logits, -jnp.inf)
    moved = jnp.where(row < n, moved, 0.0)
    l_ref[...] = logits
    m_ref[...] = moved

    @pl.when(i == 0)
    def _():
        s_ref[0:1, :] = jnp.full((1, logits.shape[1]), -jnp.inf, F32)
        s_ref[1:8, :] = jnp.zeros((7, logits.shape[1]), F32)

    old = s_ref[0:1, :]
    top = jnp.maximum(old, jnp.max(logits, axis=0, keepdims=True))
    e = jnp.exp(logits - top)
    scale = jnp.exp(old - top)
    s_ref[0:1, :] = top
    s_ref[1:2, :] = s_ref[1:2, :] * scale + jnp.sum(e, axis=0, keepdims=True)
    s_ref[2:3, :] = s_ref[2:3, :] * scale + jnp.sum(e * moved, axis=0, keepdims=True)


def fwd(h, t, w, d):
    n, k = w.shape
    tok = h.shape[1]
    whole = pl.BlockSpec((k, tok), lambda i: (0, 0))
    part = pl.BlockSpec((BLOCK, k), lambda i: (i, 0))
    res = pl.BlockSpec((BLOCK, tok), lambda i: (i, 0))
    return pl.pallas_call(
        lambda *refs: fwd_kernel(n, *refs),
        grid=(pl.cdiv(n, BLOCK),),
        in_specs=[whole, whole, part, part],
        out_specs=[res, res, pl.BlockSpec((8, tok), lambda i: (0, 0))],
        out_shape=[
            jax.ShapeDtypeStruct((n, tok), F32),
            jax.ShapeDtypeStruct((n, tok), F32),
            jax.ShapeDtypeStruct((8, tok), F32),
        ],
        compiler_params=pltpu.CompilerParams(vmem_limit_bytes=48 * 2**20),
        cost_estimate=pl.CostEstimate(
            flops=6 * n * k * tok, bytes_accessed=2 * n * k * 2 + 2 * n * tok * 4, transcendentals=n * tok
        ),
    )(h, t, w, d)


def merge(parts):
    top = parts[0][0]
    for p in parts[1:]:
        top = jnp.maximum(top, p[0])
    total = weighted = 0.0
    for p in parts:
        scale = jnp.exp(p[0] - top)
        total += p[1] * scale
        weighted += p[2] * scale
    return jnp.stack([top, total, weighted])


def per_device(hidden, tangent, head_weight, weight_dir):
    v = lax.axis_index("vocab")
    y = lax.axis_index("seq")
    z, x, c = v // (NX * NC), (v // NC) % NX, v % NC
    w, wd = head_weight.T, weight_dir.T
    n, dim = w.shape
    tok = hidden.shape[0]

    own = jnp.concatenate([hidden.T, tangent.T], axis=0)
    own = jnp.stack([own] + [vocab_shift(own, 0, k) for k in range(1, NZ)])
    own = jnp.stack([own] + [vocab_shift(own, 1, k) for k in range(1, NX)])
    other = vocab_shift(own, 2, 1)
    pos = jnp.stack([z, x, c]).astype(jnp.int32)
    h, t = order(pos, own, other, dim, tok)

    part = dim // NY
    hs = [lax.dynamic_slice_in_dim(h, y * part, part, 0)]
    for k in range(1, NY):
        hs.append(seq_shift(lax.dynamic_slice_in_dim(h, ((y - k) % NY) * part, part, 0), k))

    logits, moved, stats = fwd(h, t, w, wd)
    s = stats[:3]
    for axis, size in ((2, NC), (1, NX), (0, NZ)):
        s = merge([s] + [vocab_shift(s, axis, k) for k in range(1, size)])
    top, total, weighted = s[0:1], s[1:2], s[2:3]
    probe = (jnp.exp(logits - top) / total * (moved - weighted / total)).astype(BF16)

    half = 592
    up, down = seq_shift(probe, 1), seq_shift(probe, -1)
    far = jnp.concatenate([seq_shift(up[:half], 1), seq_shift(down[half:], -1)], axis=0)
    gw = 0.0
    for p, hk in ((probe, hs[0]), (up, hs[1]), (down, hs[3]), (far, hs[2])):
        gw += lax.dot_general(p, hk, (((1,), (1,)), ((), ())), preferred_element_type=F32)

    gh = lax.dot_general(w, probe, (((0,), (0,)), ((), ())), preferred_element_type=F32)
    gh = gh.reshape(NZ, NX, NC, dim // (NZ * NX * NC), tok)
    pick = lambda a, axis, i: lax.dynamic_index_in_dim(a, i, axis, keepdims=False)
    gh = pick(gh, 2, c) + vocab_shift(pick(gh, 2, 1 - c), 2, 1)
    gh = pick(gh, 1, x) + sum(
        vocab_shift(pick(gh, 1, (x - k) % NX).astype(BF16), 1, k).astype(F32) for k in range(1, NX)
    )
    gh = pick(gh, 0, z) + sum(vocab_shift(pick(gh, 0, (z - k) % NZ), 0, k) for k in range(1, NZ))
    return gh.T, gw.T


def solution(mesh):
    placed = (P("seq", "vocab"), P("seq", "vocab"), P(None, "vocab"), P(None, "vocab"))
    return jax.shard_map(
        per_device,
        mesh=mesh,
        in_specs=placed,
        out_specs=(P("seq", "vocab"), P("seq", "vocab")),
        check_vma=False,
    )
```

```python
import jax
import jax.numpy as jnp
from jax import lax
from jax.experimental import pallas as pl
from jax.experimental.pallas import tpu as pltpu
from jax.sharding import PartitionSpec as P

NZ, NX, NC, NY = 8, 4, 2, 4
F32, BF16 = jnp.float32, jnp.bfloat16
BLOCK = 304
HALF = 2 * BLOCK
SMEM = pl.BlockSpec(memory_space=pltpu.SMEM)
VMEM = pl.BlockSpec(memory_space=pltpu.VMEM)


def params(mib):
    return pltpu.CompilerParams(vmem_limit_bytes=mib * 2**20)


def vocab_shift(a, dim, k):
    perm = []
    for z in range(NZ):
        for x in range(NX):
            for c in range(NC):
                at = [z, x, c]
                at[dim] = (at[dim] + k) % (NZ, NX, NC)[dim]
                perm.append(((at[0] * NX + at[1]) * NC + at[2], (z * NX + x) * NC + c))
    return lax.ppermute(a, "vocab", perm)


def seq_shift(a, k):
    return lax.ppermute(a, "seq", [((y + k) % NY, y) for y in range(NY)])


def order_kernel(pos_ref, a0, a1, b0, b1, h_ref, t_ref, *send):
    x, c, y = pos_ref[0], pos_ref[1], pos_ref[2]
    for kc, (a, b) in enumerate(((a0, b0), (a1, b1))):
        for kx in range(NX):
            for zz in range(NZ):
                xx = lax.rem(x + kx, NX)
                cc = lax.rem(c + kc, NC)
                row = pl.multiple_of(zz * 256 + xx * 64 + cc * 32, 32)
                h_ref[pl.ds(row, 32), :] = a[kx, zz, 0:32, :]
                t_ref[pl.ds(row, 16), :] = a[kx, zz, 32:48, :]
                t_ref[pl.ds(row + 16, 16), :] = b[zz, kx, :, :]
    part = send[0].shape[0]
    for k, out in enumerate(send):
        out[...] = h_ref[pl.ds(pl.multiple_of(lax.rem(y + k, NY) * part, part), part), :]


def order(pos, a0, a1, b0, b1, dim, tok):
    out = [jax.ShapeDtypeStruct((dim, tok), BF16)] * 2 + [jax.ShapeDtypeStruct((dim // NY, tok), BF16)] * NY
    return pl.pallas_call(
        order_kernel,
        out_shape=out,
        in_specs=[SMEM] + [VMEM] * 4,
        out_specs=[VMEM] * len(out),
        compiler_params=params(40),
        cost_estimate=pl.CostEstimate(flops=0, bytes_accessed=10 * 2**20, transcendentals=0),
    )(pos, a0, a1, b0, b1)


def fwd_kernel(n, h_ref, t_ref, w_ref, d_ref, l_ref, m_ref, s_ref):
    i = pl.program_id(0)
    w = w_ref[...]
    h = h_ref[...]
    logits = jnp.dot(w, h, preferred_element_type=F32)
    moved = jnp.dot(w, t_ref[...], preferred_element_type=F32) + jnp.dot(
        d_ref[...], h, preferred_element_type=F32
    )
    row = lax.broadcasted_iota(jnp.int32, logits.shape, 0) + i * BLOCK
    logits = jnp.where(row < n, logits, -jnp.inf)
    moved = jnp.where(row < n, moved, 0.0)
    l_ref[...] = logits
    m_ref[...] = moved

    @pl.when(i == 0)
    def _():
        s_ref[0:1, :] = jnp.full((1, logits.shape[1]), -jnp.inf, F32)
        s_ref[1:3, :] = jnp.zeros((2, logits.shape[1]), F32)

    old = s_ref[0:1, :]
    top = jnp.maximum(old, jnp.max(logits, axis=0, keepdims=True))
    e = jnp.exp(logits - top)
    scale = jnp.exp(old - top)
    s_ref[0:1, :] = top
    s_ref[1:2, :] = s_ref[1:2, :] * scale + jnp.sum(e, axis=0, keepdims=True)
    s_ref[2:3, :] = s_ref[2:3, :] * scale + jnp.sum(e * moved, axis=0, keepdims=True)


def fwd(h, t, w, d):
    n, k = w.shape
    tok = h.shape[1]
    whole = pl.BlockSpec((k, tok), lambda i: (0, 0))
    part = pl.BlockSpec((BLOCK, k), lambda i: (i, 0))
    res = pl.BlockSpec((BLOCK, tok), lambda i: (i, 0))
    return pl.pallas_call(
        lambda *refs: fwd_kernel(n, *refs),
        grid=(pl.cdiv(n, BLOCK),),
        in_specs=[whole, whole, part, part],
        out_specs=[res, res, pl.BlockSpec((3, tok), lambda i: (0, 0))],
        out_shape=[
            jax.ShapeDtypeStruct((n, tok), F32),
            jax.ShapeDtypeStruct((n, tok), F32),
            jax.ShapeDtypeStruct((3, tok), F32),
        ],
        compiler_params=params(48),
        cost_estimate=pl.CostEstimate(
            flops=6 * n * k * tok, bytes_accessed=2 * n * k * 2 + 2 * n * tok * 4, transcendentals=n * tok
        ),
    )(h, t, w, d)


def probe_kernel(s_ref, l_ref, m_ref, a_ref, b_ref, k_ref):
    i = pl.program_id(0)

    @pl.when(i == 0)
    def _():
        tops = s_ref[:, 0, :]
        top = jnp.max(tops, axis=0, keepdims=True)
        scale = jnp.exp(tops - top)
        total = jnp.sum(s_ref[:, 1, :] * scale, axis=0, keepdims=True)
        k_ref[0:1, :] = top
        k_ref[1:2, :] = 1.0 / total
        k_ref[2:3, :] = jnp.sum(s_ref[:, 2, :] * scale, axis=0, keepdims=True) / total

    probe = jnp.exp(l_ref[...] - k_ref[0:1, :]) * k_ref[1:2, :] * (m_ref[...] - k_ref[2:3, :])

    @pl.when(i < 2)
    def _():
        a_ref[...] = probe.astype(BF16)

    @pl.when(i >= 2)
    def _():
        b_ref[...] = probe.astype(BF16)


def probe_of(stats, logits, moved):
    n, tok = logits.shape
    part = pl.BlockSpec((BLOCK, tok), lambda i: (i, 0))
    return pl.pallas_call(
        probe_kernel,
        grid=(pl.cdiv(n, BLOCK),),
        in_specs=[pl.BlockSpec(stats.shape, lambda i: (0, 0, 0)), part, part],
        out_specs=[
            pl.BlockSpec((BLOCK, tok), lambda i: (jnp.minimum(i, 1), 0)),
            pl.BlockSpec((BLOCK, tok), lambda i: (jnp.maximum(i - 2, 0), 0)),
        ],
        out_shape=[jax.ShapeDtypeStruct((HALF, tok), BF16), jax.ShapeDtypeStruct((n - HALF, tok), BF16)],
        scratch_shapes=[pltpu.VMEM((8, tok), F32)],
        compiler_params=params(32),
        cost_estimate=pl.CostEstimate(flops=4 * n * tok, bytes_accessed=10 * n * tok, transcendentals=n * tok),
    )(stats, logits, moved)


def weight_kernel(*refs):
    out = refs[-1]
    probes, hidden = refs[:8], refs[8:12]
    half = probes[0].shape[0]
    dims = (((1,), (1,)), ((), ()))
    for lo, hi, part in ((0, half, probes[0::2]), (half, out.shape[0], probes[1::2])):
        acc = lax.dot_general(part[0][...], hidden[0][...], dims, preferred_element_type=F32)
        for p, h in zip(part[1:], hidden[1:]):
            acc += lax.dot_general(p[...], h[...], dims, preferred_element_type=F32)
        out[lo:hi, :] = acc


def weight(probes, hidden, n):
    part, tok = hidden[0].shape
    step = part // 2
    return pl.pallas_call(
        weight_kernel,
        grid=(2,),
        in_specs=[pl.BlockSpec(p.shape, lambda i: (0, 0)) for p in probes]
        + [pl.BlockSpec((step, tok), lambda i: (i, 0))] * NY,
        out_specs=pl.BlockSpec((n, step), lambda i: (0, i)),
        out_shape=jax.ShapeDtypeStruct((n, part), F32),
        compiler_params=params(40),
        cost_estimate=pl.CostEstimate(
            flops=2 * n * part * tok * NY, bytes_accessed=4 * n * part + 2 * NY * (n + part) * tok, transcendentals=0
        ),
    )(*probes, *hidden)


def rows_kernel(pos_ref, a_ref, b_ref, w_ref, own_ref, other_ref, res_ref):
    c = pos_ref[1]
    dims = (((0,), (0,)), ((), ()))
    res = lax.dot_general(w_ref[0:HALF, :], a_ref[...], dims, preferred_element_type=F32)
    res_ref[...] = res + lax.dot_general(w_ref[HALF:, :], b_ref[...], dims, preferred_element_type=F32)
    for xx in range(NX):
        for out, cc in ((own_ref, c), (other_ref, 1 - c)):
            out[0, xx] = res_ref[pl.ds(pl.multiple_of((xx * NC + cc) * 32, 32), 32), :]


def rows(pos, a, b, w):
    n, dim = w.shape
    tok = a.shape[1]
    per = dim // NZ
    return pl.pallas_call(
        rows_kernel,
        grid=(NZ,),
        in_specs=[
            SMEM,
            pl.BlockSpec((HALF, tok), lambda i: (0, 0)),
            pl.BlockSpec((n - HALF, tok), lambda i: (0, 0)),
            pl.BlockSpec((n, per), lambda i: (0, i)),
        ],
        out_specs=[pl.BlockSpec((1, NX, 32, tok), lambda i: (i, 0, 0, 0))] * 2,
        out_shape=[jax.ShapeDtypeStruct((NZ, NX, 32, tok), F32)] * 2,
        scratch_shapes=[pltpu.VMEM((per, tok), F32)],
        compiler_params=params(32),
        cost_estimate=pl.CostEstimate(
            flops=2 * n * dim * tok, bytes_accessed=2 * n * dim + 4 * dim * tok, transcendentals=0
        ),
    )(pos, a, b, w)


Z_GROUPS = [[(z * NX + x) * NC + c for z in range(NZ)] for x in range(NX) for c in range(NC)]
ZX_GROUPS = [[(z * NX + x) * NC + c for z in range(NZ) for x in range(NX)] for c in range(NC)]


def exchange(a, groups=None):
    return lax.all_to_all(a, "vocab", 0, 0, axis_index_groups=groups, tiled=True)


def spread(a, groups, size):
    return exchange(jnp.broadcast_to(a[None], (size,) + a.shape), groups)


def per_device(hidden, tangent, head_weight, weight_dir):
    v = lax.axis_index("vocab")
    y = lax.axis_index("seq")
    x, c = (v // NC) % NX, v % NC
    pos = jnp.stack([x, c, y]).astype(jnp.int32)
    w, wd = head_weight.T, weight_dir.T
    n, dim = w.shape
    tok = hidden.shape[0]

    ht, tt = hidden.T, tangent.T
    a = jnp.concatenate([ht, tt[:16]], axis=0)
    b = tt[16:]
    b = jnp.stack([b] + [vocab_shift(b, 1, k) for k in range(1, NX)])
    a, b = lax.optimization_barrier((spread(a, Z_GROUPS, NZ), b))
    a = [a] + [vocab_shift(a, 1, k) for k in range(1, NX)]
    *a, b = lax.optimization_barrier((*a, spread(b, Z_GROUPS, NZ)))
    a = jnp.stack(a)
    b2 = vocab_shift(b, 2, 1)
    a2 = vocab_shift(a, 2, 1)
    h, t, *send = order(pos, a, a2, b, b2, dim, tok)
    hs = [send[0]] + [seq_shift(send[k], -k) for k in range(1, NY)]

    logits, moved, stats = fwd(h, t, w, wd)
    stats = spread(stats, None, NZ * NX * NC)
    stats, *hs = lax.optimization_barrier((stats, *hs))
    pa, pb = probe_of(stats, logits, moved)

    up_a, down_b = seq_shift(pa, 1), seq_shift(pb, -1)
    own, other = rows(pos, pa, pb, w)
    late_a, late_b, other = lax.optimization_barrier((pa, pb, other))
    up_b, down_a = seq_shift(late_b, 1), seq_shift(late_a, -1)
    gh = (own + vocab_shift(other, 2, 1)).astype(BF16)
    up_a, down_b, gh = lax.optimization_barrier((up_a, down_b, gh))
    far_a, far_b = seq_shift(up_a, 1), seq_shift(down_b, -1)
    gh = exchange(gh.reshape(NZ * NX, 32, tok), ZX_GROUPS)
    far_a, far_b, gh = lax.optimization_barrier((far_a, far_b, gh))
    gh = jnp.sum(gh.astype(F32), axis=0)
    gw = weight([pa, pb, up_a, up_b, down_a, down_b, far_a, far_b], [hs[0], hs[3], hs[1], hs[2]], n)
    return gh.T, gw.T


def solution(mesh):
    placed = (P("seq", "vocab"), P("seq", "vocab"), P(None, "vocab"), P(None, "vocab"))
    return jax.shard_map(
        per_device,
        mesh=mesh,
        in_specs=placed,
        out_specs=(P("seq", "vocab"), P("seq", "vocab")),
        check_vma=False,
    )
```

```python
import jax
import jax.numpy as jnp
from jax import lax
from jax.experimental import pallas as pl
from jax.experimental.pallas import tpu as pltpu
from jax.sharding import PartitionSpec as P

NZ, NX, NC, NY = 8, 4, 2, 4
F32, BF16 = jnp.float32, jnp.bfloat16
BLOCK = 400
HALF = 608
SMEM = pl.BlockSpec(memory_space=pltpu.SMEM)
VMEM = pl.BlockSpec(memory_space=pltpu.VMEM)


def params(mib):
    return pltpu.CompilerParams(vmem_limit_bytes=mib * 2**20)


def receive(a, pair=0, quad=0, x=0, core=0):
    perm = []
    for i in range(NZ * NX * NC):
        q, p, xx, c = i // 16, i // 8 % 2, i // 2 % 4, i % 2
        src = (((q + quad) % 4 * 2 + (p + pair) % 2) * NX + (xx + x) % NX) * NC + (c + core) % NC
        perm.append((src, i))
    return lax.ppermute(a, "vocab", perm)


def seq_shift(a, k):
    return lax.ppermute(a, "seq", [((y + k) % NY, y) for y in range(NY)])


def stack_kernel(*refs):
    *parts, out = refs
    for k, part in enumerate(parts):
        out[k] = part[...]


def stack(parts):
    out = (len(parts),) + parts[0].shape
    return pl.pallas_call(
        stack_kernel,
        in_specs=[VMEM] * len(parts),
        out_specs=VMEM,
        out_shape=jax.ShapeDtypeStruct(out, parts[0].dtype),
        compiler_params=params(4),
        cost_estimate=pl.CostEstimate(flops=0, bytes_accessed=4 * len(parts) * parts[0].size, transcendentals=0),
    )(*parts)


def fill(out, pos_ref, own, other):
    x, c = pos_ref[0], pos_ref[1]
    for src, cc in ((own, c), (other, 1 - c)):
        for kx in range(NX):
            for zz in range(NZ):
                row = zz * 256 + lax.rem(x + kx, NX) * 64 + cc * 32
                out[pl.ds(pl.multiple_of(row, 32), 32), :] = src[kx, zz]


def pick_kernel(pos_ref, own, *outs):
    x, y = pos_ref[0], pos_ref[2]
    for k, out in enumerate(outs):
        place = lax.rem(y + k + 1, NY) * (NZ // NY)
        for kx in range(NX):
            for j in range(NZ // NY):
                row = j * 128 + lax.rem(x + kx, NX) * 32
                out[pl.ds(pl.multiple_of(row, 32), 32), :] = own[kx, place + j]


def pick(pos, own):
    tok = own.shape[-1]
    return pl.pallas_call(
        pick_kernel,
        in_specs=[SMEM, VMEM],
        out_specs=[VMEM] * (NY - 1),
        out_shape=[jax.ShapeDtypeStruct((NZ * 128 // NY, tok), BF16)] * (NY - 1),
        compiler_params=params(8),
        cost_estimate=pl.CostEstimate(flops=0, bytes_accessed=2 * 2**20, transcendentals=0),
    )(pos, own)


def first_kernel(pos_ref, own, other, w_ref, d_ref, l_ref, m_ref, mine_ref, h_ref):
    @pl.when(pl.program_id(0) == 0)
    def _():
        fill(h_ref, pos_ref, own, other)
        part = mine_ref.shape[0]
        mine_ref[...] = h_ref[pl.ds(pl.multiple_of(pos_ref[2] * part, part), part), :]

    h = h_ref[...]
    l_ref[...] = jnp.dot(w_ref[...], h, preferred_element_type=F32)
    m_ref[...] = jnp.dot(d_ref[...], h, preferred_element_type=F32)


def first(pos, own, other, w, d):
    n, k = w.shape
    tok = own.shape[-1]
    whole = pl.BlockSpec(own.shape, lambda i: (0, 0, 0, 0))
    part = pl.BlockSpec((BLOCK, k), lambda i: (i, 0))
    res = pl.BlockSpec((BLOCK, tok), lambda i: (i, 0))
    return pl.pallas_call(
        first_kernel,
        grid=(pl.cdiv(n, BLOCK),),
        in_specs=[SMEM, whole, whole, part, part],
        out_specs=[res, res, pl.BlockSpec((k // NY, tok), lambda i: (0, 0))],
        out_shape=[jax.ShapeDtypeStruct((n, tok), F32)] * 2 + [jax.ShapeDtypeStruct((k // NY, tok), BF16)],
        scratch_shapes=[pltpu.VMEM((k, tok), BF16)],
        compiler_params=params(48),
        cost_estimate=pl.CostEstimate(
            flops=4 * n * k * tok, bytes_accessed=4 * n * k + 8 * n * tok, transcendentals=0
        ),
    )(pos, own, other, w, d)


def second_kernel(n, pos_ref, own, other, w_ref, l_ref, p_ref, m_ref, o_ref, t_ref, s_ref):
    i = pl.program_id(0)
    tok = t_ref.shape[1]

    @pl.when(i == 0)
    def _():
        fill(t_ref, pos_ref, own, other)
        s_ref[0:1, :] = jnp.full((1, tok), -jnp.inf, F32)
        s_ref[1:8, :] = jnp.zeros((7, tok), F32)

    moved = jnp.dot(w_ref[...], t_ref[...], preferred_element_type=F32) + p_ref[...]
    m_ref[...] = moved
    row = lax.broadcasted_iota(jnp.int32, moved.shape, 0) + i * BLOCK
    logits = jnp.where(row < n, l_ref[...], -jnp.inf)
    moved = jnp.where(row < n, moved, 0.0)
    old = s_ref[0:1, :]
    top = jnp.maximum(old, jnp.max(logits, axis=0, keepdims=True))
    e = jnp.exp(logits - top)
    scale = jnp.exp(old - top)
    s_ref[0:1, :] = top
    s_ref[1:2, :] = s_ref[1:2, :] * scale + jnp.sum(e, axis=0, keepdims=True)
    s_ref[2:3, :] = s_ref[2:3, :] * scale + jnp.sum(e * moved, axis=0, keepdims=True)

    @pl.when(i == pl.num_programs(0) - 1)
    def _():
        for k in range(o_ref.shape[0]):
            o_ref[k] = s_ref[0:3, :]


def second(pos, own, other, w, logits, partial):
    n, k = w.shape
    tok = own.shape[-1]
    whole = pl.BlockSpec(own.shape, lambda i: (0, 0, 0, 0))
    res = pl.BlockSpec((BLOCK, tok), lambda i: (i, 0))
    return pl.pallas_call(
        lambda *refs: second_kernel(n, *refs),
        grid=(pl.cdiv(n, BLOCK),),
        in_specs=[SMEM, whole, whole, pl.BlockSpec((BLOCK, k), lambda i: (i, 0)), res, res],
        out_specs=[res, pl.BlockSpec((8, 3, tok), lambda i: (0, 0, 0))],
        out_shape=[jax.ShapeDtypeStruct((n, tok), F32), jax.ShapeDtypeStruct((8, 3, tok), F32)],
        scratch_shapes=[pltpu.VMEM((k, tok), BF16), pltpu.VMEM((8, tok), F32)],
        compiler_params=params(24),
        cost_estimate=pl.CostEstimate(
            flops=2 * n * k * tok, bytes_accessed=2 * n * k + 12 * n * tok, transcendentals=n * tok
        ),
    )(pos, own, other, w, logits, partial)


def merged(s_ref):
    tops = s_ref[:, 0, :]
    top = jnp.max(tops, axis=0, keepdims=True)
    scale = jnp.exp(tops - top)
    total = jnp.sum(s_ref[:, 1, :] * scale, axis=0, keepdims=True)
    return top, total, jnp.sum(s_ref[:, 2, :] * scale, axis=0, keepdims=True)


def merge_kernel(s_ref, o_ref):
    for at, value in enumerate(merged(s_ref)):
        for k in range(o_ref.shape[0]):
            o_ref[k, at : at + 1, :] = value


def merge(stats):
    return pl.pallas_call(
        merge_kernel,
        in_specs=[VMEM],
        out_specs=VMEM,
        out_shape=jax.ShapeDtypeStruct(stats.shape, F32),
        compiler_params=params(4),
    )(stats)


def probe_kernel(s_ref, l_ref, m_ref, p_ref, k_ref):
    @pl.when(pl.program_id(0) == 0)
    def _():
        top, total, weighted = merged(s_ref)
        k_ref[0:1, :] = top
        k_ref[1:2, :] = 1.0 / total
        k_ref[2:3, :] = weighted / total

    p_ref[...] = (jnp.exp(l_ref[...] - k_ref[0:1, :]) * k_ref[1:2, :] * (m_ref[...] - k_ref[2:3, :])).astype(BF16)


def probe_of(stats, logits, moved):
    n, tok = logits.shape
    part = pl.BlockSpec((BLOCK, tok), lambda i: (i, 0))
    return pl.pallas_call(
        probe_kernel,
        grid=(pl.cdiv(n, BLOCK),),
        in_specs=[pl.BlockSpec(stats.shape, lambda i: (0, 0, 0)), part, part],
        out_specs=part,
        out_shape=jax.ShapeDtypeStruct((n, tok), BF16),
        scratch_shapes=[pltpu.VMEM((8, tok), F32)],
        compiler_params=params(16),
        cost_estimate=pl.CostEstimate(flops=4 * n * tok, bytes_accessed=10 * n * tok, transcendentals=n * tok),
    )(stats, logits, moved)


def turn_kernel(up, down, own, other, x1, x2, x3, far_a, far_b, keep, away):
    far_a[...] = up[0:HALF, :]
    far_b[...] = down[HALF:, :]
    for z in range(NZ):
        total = own[z] + other[0, z]
        for part in (x1, x2, x3):
            total += part[z].astype(F32)
        if z < NZ // 2:
            keep[z] = total
        else:
            away[z - NZ // 2] = total


def turn(up, down, own, other, from_x):
    n, tok = up.shape
    half = (NZ // 2,) + own.shape[1:]
    return pl.pallas_call(
        turn_kernel,
        in_specs=[VMEM] * 7,
        out_specs=[VMEM] * 4,
        out_shape=[
            jax.ShapeDtypeStruct((HALF, tok), BF16),
            jax.ShapeDtypeStruct((n - HALF, tok), BF16),
            jax.ShapeDtypeStruct(half, F32),
            jax.ShapeDtypeStruct(half, F32),
        ],
        compiler_params=params(8),
        cost_estimate=pl.CostEstimate(flops=0, bytes_accessed=4 * n * tok, transcendentals=0),
    )(up, down, own, other, *from_x)


NT = (((1,), (1,)), ((), ()))


def near_kernel(pos_ref, probe, up, down, mine, r_down, r_far, r_up, q, acc, far, h_ref):
    c = pos_ref[1]
    for k, (own, out) in enumerate(((r_down, h_ref.at[0]), (r_far, far), (r_up, h_ref.at[1]))):
        for i in range(own.shape[0] // 32):
            lo, hi = i * 32, i * 32 + 32
            out[pl.ds(pl.multiple_of(lo * 2 + c * 32, 32), 32), :] = own[lo:hi, :]
            out[pl.ds(pl.multiple_of(lo * 2 + (1 - c) * 32, 32), 32), :] = q[k, lo:hi, :]
    for lo, hi in ((0, HALF), (HALF, acc.shape[0])):
        total = lax.dot_general(probe[lo:hi, :], mine[...], NT, preferred_element_type=F32)
        total += lax.dot_general(down[lo:hi, :], h_ref[0], NT, preferred_element_type=F32)
        acc[lo:hi, :] = total + lax.dot_general(up[lo:hi, :], h_ref[1], NT, preferred_element_type=F32)


def near_weight(pos, probes, mine, received, swapped):
    n = probes[0].shape[0]
    part, tok = mine.shape
    return pl.pallas_call(
        near_kernel,
        in_specs=[SMEM] + [VMEM] * 8,
        out_specs=[VMEM] * 2,
        out_shape=[jax.ShapeDtypeStruct((n, part), F32), jax.ShapeDtypeStruct((part, tok), BF16)],
        scratch_shapes=[pltpu.VMEM((2, part, tok), BF16)],
        compiler_params=params(20),
        cost_estimate=pl.CostEstimate(flops=6 * n * part * tok, bytes_accessed=10 * n * part, transcendentals=0),
    )(pos, *probes, mine, *received, swapped)


def far_kernel(acc, far_a, far_b, hidden, out):
    out[0:HALF, :] = acc[0:HALF, :] + lax.dot_general(far_a[...], hidden[...], NT, preferred_element_type=F32)
    out[HALF:, :] = acc[HALF:, :] + lax.dot_general(far_b[...], hidden[...], NT, preferred_element_type=F32)


def far_weight(acc, far_a, far_b, hidden):
    n, part = acc.shape
    return pl.pallas_call(
        far_kernel,
        in_specs=[VMEM] * 4,
        out_specs=VMEM,
        out_shape=jax.ShapeDtypeStruct((n, part), F32),
        compiler_params=params(16),
        cost_estimate=pl.CostEstimate(flops=2 * n * part * part, bytes_accessed=10 * n * part, transcendentals=0),
    )(acc, far_a, far_b, hidden)


def rows_kernel(pos_ref, p_ref, w_ref, own_ref, rest_ref, *refs):
    *other, res_ref = refs
    x, c = pos_ref[0], pos_ref[1]
    res_ref[...] = lax.dot_general(w_ref[...], p_ref[...], (((0,), (0,)), ((), ())), preferred_element_type=F32)
    each = NX // len(other)
    for kx in range(NX):
        row = lax.rem(x + kx, NX) * 64
        out, at = (rest_ref, kx - 1) if kx else (own_ref, 0)
        out[at, 0] = res_ref[pl.ds(pl.multiple_of(row + c * 32, 32), 32), :]
        out = other[kx // each]
        out[kx % each, 0] = res_ref[pl.ds(pl.multiple_of(row + (1 - c) * 32, 32), 32), :]


def rows(pos, p, w):
    n, dim = w.shape
    tok = p.shape[1]
    per = dim // NZ
    counts = [1, NX - 1, NX // 2, NX // 2]

    def z_block(i, pos_ref):
        z = pos_ref[3]
        return (0, lax.rem(z // 2 + i % 4, 4) * 2 + lax.rem(z % 2 + i // 4, 2))

    return pl.pallas_call(
        rows_kernel,
        grid_spec=pltpu.PrefetchScalarGridSpec(
            num_scalar_prefetch=1,
            grid=(NZ,),
            in_specs=[
                pl.BlockSpec(p.shape, lambda i, pos_ref: (0, 0)),
                pl.BlockSpec((n, per), z_block),
            ],
            out_specs=[pl.BlockSpec((m, 1, 32, tok), lambda i, pos_ref: (0, i, 0, 0)) for m in counts],
            scratch_shapes=[pltpu.VMEM((per, tok), F32)],
        ),
        out_shape=[jax.ShapeDtypeStruct((m, NZ, 32, tok), F32) for m in counts],
        compiler_params=params(16),
        cost_estimate=pl.CostEstimate(
            flops=2 * n * dim * tok, bytes_accessed=2 * n * dim + 4 * dim * tok, transcendentals=0
        ),
    )(pos, p, w)


Z_GROUPS = [[(z * NX + x) * NC + c for z in range(NZ)] for x in range(NX) for c in range(NC)]

XC_GROUPS = [[z * NX * NC + i for i in range(NX * NC)] for z in range(NZ)]


def exchange(a, groups):
    return lax.all_to_all(a, "vocab", 0, 0, axis_index_groups=groups, tiled=True)


def per_device(hidden, tangent, head_weight, weight_dir):
    v = lax.axis_index("vocab")
    y = lax.axis_index("seq")
    pos = jnp.stack([(v // NC) % NX, v % NC, y, v // (NX * NC)]).astype(jnp.int32)
    w, wd = head_weight.T, weight_dir.T

    both = jnp.stack([hidden.T, tangent.T])
    both = exchange(jnp.broadcast_to(both[None], (NZ,) + both.shape), Z_GROUPS)
    a, b = both[:, 0], both[:, 1]
    a = [a] + [receive(a, x=k) for k in range(1, NX)]
    b = [b] + [receive(b, x=k) for k in range(1, NX)]
    a0 = stack(a)
    a1 = receive(a0, core=1)
    to_up, to_far, to_down = pick(pos, a0)
    r_down, r_up = seq_shift(to_up, -1), seq_shift(to_down, 1)
    logits, partial, mine = first(pos, a0, a1, w, wd)
    partial, b, r_down, r_up, to_far = lax.optimization_barrier((partial, b, r_down, r_up, to_far))
    b0 = stack(b)
    b1 = receive(b0, core=1)
    r_far = seq_shift(to_far, 2)
    moved, stats = second(pos, b0, b1, w, logits, partial)
    stats, r_far = lax.optimization_barrier((stats, r_far))
    swapped = receive(stack([r_down, r_far, r_up]), core=1)
    stats = merge(exchange(stats, XC_GROUPS))
    stats, swapped = lax.optimization_barrier((stats, swapped))
    stats = exchange(stats, Z_GROUPS)
    probe = probe_of(stats, logits, moved)

    up, down = seq_shift(probe, 1), seq_shift(probe, -1)
    own, rest, *other = rows(pos, probe, w)
    other = [receive(o, core=1) for o in other]
    from_x = []
    for k in range(1, NX):
        part = rest[k - 1] + other[k // 2][k % 2]
        from_x.append(receive(part.astype(BF16), x=-k))
    far_a, far_b, gh, away = turn(up, down, own[0], other[0], from_x)
    far_a, far_b = seq_shift(far_a, 1), seq_shift(far_b, -1)
    gh = gh + receive(away, pair=1)
    gh = gh[0] + sum(receive(gh[k], quad=-k) for k in range(1, 4))
    acc, far = near_weight(pos, [probe, up, down], mine, [r_down, r_far, r_up], swapped)
    gw = far_weight(acc, far_a, far_b, far)
    return gh.T, gw.T


def solution(mesh):
    placed = (P("seq", "vocab"), P("seq", "vocab"), P(None, "vocab"), P(None, "vocab"))
    return jax.shard_map(
        per_device,
        mesh=mesh,
        in_specs=placed,
        out_specs=(P("seq", "vocab"), P("seq", "vocab")),
        check_vma=False,
    )
```
